32 devices in a mesh: fsdp: 4 (over z), ctx: 8 (over y, x, core).
Axes of the slice: x: 2, y: 2, z: 4, core: 2. Of those that a mesh axis runs over, the one named last changes fastest.
Arguments:
- hidden_in: bfloat16 [8, 2048, 1024], P('fsdp', 'ctx'), may hold values from -6 to 6
- cotangent: bfloat16 [8, 2048, 1024], P('fsdp', 'ctx'), may hold values from -6 to 6
- segments: int32 [8, 2048], P('fsdp'), may hold values from 0 to 3, as said below
- entry_gain: bfloat16 [1024], P('fsdp'), may hold values from 0.5 to 1.5
- query_weight: bfloat16 [1024, 512], P('fsdp'), may hold values from -0.1875 to 0.1875
- key_weight: bfloat16 [1024, 128], P('fsdp'), may hold values from -0.1875 to 0.1875
- value_weight: bfloat16 [1024, 128], P('fsdp'), may hold values from -0.1875 to 0.1875
- output_weight: bfloat16 [512, 1024], P('fsdp'), may hold values from -1.5 to 1.5
- mixer_weight: bfloat16 [1024, 3328], P('fsdp'), may hold values from -0.1875 to 0.1875
- step_weight: bfloat16 [1024, 24], P('fsdp'), may hold values from -0.1875 to 0.1875
- conv_weight: bfloat16 [4, 1792], P(None, 'fsdp'), may hold values from -3 to 3
- conv_bias: bfloat16 [1792], P('fsdp'), may hold values from -3 to 3
- step_offset: bfloat16 [24], P('fsdp'), may hold values from -1 to 1
- decay_rate: bfloat16 [24], P('fsdp'), may hold values from 0 to 1, as said below
- skip_weight: bfloat16 [24], P('fsdp'), may hold values from -1 to 1
- gated_gain: bfloat16 [1536], P('fsdp'), may hold values from 0.5 to 1.5
- merge_weight: bfloat16 [1536, 1024], P('fsdp'), may hold values from -0.15625 to 0.15625
- second_gain: bfloat16 [1024], P('fsdp'), may hold values from 0.5 to 1.5
- gate_weight: bfloat16 [1024, 2048], P('fsdp'), may hold values from -0.1875 to 0.1875
- up_weight: bfloat16 [1024, 2048], P('fsdp'), may hold values from -0.1875 to 0.1875
- down_weight: bfloat16 [2048, 1024], P('fsdp'), may hold values from -0.125 to 0.125
Outputs:
- block_out: float32 [8, 2048, 1024], P('fsdp', 'ctx')
- tokens_grad: float32 [8, 2048, 1024], P('fsdp', 'ctx')
- entry_grad: float32 [1024], P('fsdp')
- query_grad: float32 [1024, 512], P('fsdp')
- key_grad: float32 [1024, 128], P('fsdp')
- value_grad: float32 [1024, 128], P('fsdp')
- output_grad: float32 [512, 1024], P('fsdp')
- mixer_grad: float32 [1024, 3328], P('fsdp')
- step_grad: float32 [1024, 24], P('fsdp')
- conv_grad: float32 [4, 1792], P(None, 'fsdp')
- bias_grad: float32 [1792], P('fsdp')
- offset_grad: float32 [24], P('fsdp')
- decay_grad: float32 [24], P('fsdp')
- skip_grad: float32 [24], P('fsdp')
- gated_grad: float32 [1536], P('fsdp')
- merge_grad: float32 [1536, 1024], P('fsdp')
- second_grad: float32 [1024], P('fsdp')
- gate_grad: float32 [1024, 2048], P('fsdp')
- up_grad: float32 [1024, 2048], P('fsdp')
- down_grad: float32 [2048, 1024], P('fsdp')
The draws below stay inside these ranges and needn't reach their ends.
Inputs may be any that keep to these rules, and one draw needn't show every extreme that they name: `segments`: within each sequence the numbers start at 0, never fall and rise by at most one from a token to the next; every document has 204 tokens or more; of each 2 consecutive sequences one is a single document, and every other sequence holds four documents. `decay_rate`: per-head rates between 0.1 / 2048 and 64 / 2048.
All inputs are finite; a program needn't handle non-finite values.
Results may differ from the reference program's by a relative error of at most 0.019.
The reference program's roundings to bfloat16 on the way count: a program that leaves them out, or rounds other values in their place, can miss the bound.
Values may be sent and summed in bfloat16 or wider, within the bound.
A program may use at most 384 MiB of HBM per device.

```python
import math
import jax
import jax.numpy as jnp
from jax import lax

D = 1024
QHEADS = 8
KVHEADS = 2
HEAD = 64
MHEADS = 24
MHEAD = 64
STATE = 128
CONVW = 4
FF = 2048
SEQ_LEN = 2048
MICRO = 2
STRETCH = 256
SEQS = 8
QW = 512
KW = 128
DS = 1536
CONV_CH = 1792
PROJ = 3328


def draw_segments(key, part):
    key = jax.random.fold_in(key, 11)
    choose_key = jax.random.fold_in(key, 1)
    cut_key = jax.random.fold_in(key, 2)
    least_gap = SEQ_LEN // 10
    chosen = jax.random.randint(choose_key, (SEQS // MICRO,), 0, MICRO)
    spare = SEQ_LEN - 4 * least_gap + 1
    raw_cuts = jnp.sort(jax.random.randint(cut_key, (SEQS, 3), 0, spare), axis=-1)
    cuts = raw_cuts + least_gap * jnp.arange(1, 4, dtype=jnp.int32)[None, :]
    places = jnp.arange(SEQ_LEN, dtype=jnp.int32)
    numbers = jnp.sum((cuts[:, None, :] <= places[None, :, None]).astype(jnp.int32), axis=-1)
    single = jnp.arange(SEQS, dtype=jnp.int32) % MICRO == jnp.repeat(chosen, MICRO)
    return jnp.where(single[:, None], 0, numbers).astype(jnp.int32)


def draw_decay_rate(key, part):
    key = jax.random.fold_in(key, 23)
    lowest, highest = (0.2, 64.0)
    spread = jax.random.uniform(key, (MHEADS,), jnp.float32)
    return (jnp.exp(math.log(lowest) + spread * (math.log(highest) - math.log(lowest))) / SEQ_LEN).astype(jnp.bfloat16)


def steps_of(own_key, shape, cuts, least, high):
    def one(dim, blocks):
        draws = jax.random.uniform(jax.random.fold_in(jax.random.fold_in(own_key, 6), dim), (blocks,), jnp.float32, least / len(cuts), high / len(cuts))
        return jnp.repeat(jnp.exp(draws), shape[dim] // blocks).reshape((-1,) + (1,) * (len(shape) - dim - 1))

    loudness = one(*cuts[0])
    for cut in cuts[1:]:
        loudness = loudness * one(*cut)
    return loudness


def gaussian(key, shape, width, limit, shards=(), kind=jnp.bfloat16):
    factor_of = steps_of(key, shape, shards, -0.22, 0.18) if shards else 1.0
    drawn = jax.random.normal(key, shape, jnp.float32) * width * factor_of
    return jnp.minimum(jnp.maximum(drawn, -limit), limit).astype(kind)


def setup_inputs(seed: int = 0) -> dict:
    keys = jax.random.split(jax.random.key(seed), 22)
    return {
        "hidden_in": gaussian(keys[0], (SEQS, SEQ_LEN, D), 1.0, 6.0, ((0, 4), (1, 8))),
        "cotangent": gaussian(keys[1], (SEQS, SEQ_LEN, D), 1.0, 6.0, ((0, 4), (1, 8))),
        "segments": draw_segments(jax.random.fold_in(keys[21], 71), 0),
        "entry_gain": jnp.clip(1.0 + 0.1 * jax.random.normal(keys[3], (D,), jnp.float32), 0.5, 1.5).astype(jnp.bfloat16),
        "query_weight": gaussian(keys[4], (D, QW), D ** -0.5, 0.1875, ((0, 4),)),
        "key_weight": gaussian(keys[5], (D, KW), D ** -0.5, 0.1875, ((0, 4),)),
        "value_weight": gaussian(keys[6], (D, KW), D ** -0.5, 0.1875, ((0, 4),)),
        "output_weight": gaussian(keys[7], (QW, D), (QW // 32) ** -0.5, 1.5, ((0, 4),)),
        "mixer_weight": gaussian(keys[8], (D, PROJ), D ** -0.5, 0.1875, ((0, 4),)),
        "step_weight": gaussian(keys[9], (D, MHEADS), D ** -0.5, 0.1875, ((0, 4),)),
        "conv_weight": gaussian(keys[10], (CONVW, CONV_CH), CONVW ** -0.5, 3.0, ((1, 4),)),
        "conv_bias": gaussian(keys[11], (CONV_CH,), 0.5, 3.0, ((0, 4),)),
        "step_offset": jnp.clip(jax.random.uniform(keys[12], (MHEADS,), jnp.float32, -1.0, 1.0) * steps_of(keys[12], (MHEADS,), ((0, 4),), -0.4, 0.0), -1.0, 1.0).astype(jnp.bfloat16),
        "decay_rate": draw_decay_rate(jax.random.fold_in(keys[21], 71), 0),
        "skip_weight": jnp.clip(jax.random.uniform(keys[14], (MHEADS,), jnp.float32, -1.0, 1.0) * steps_of(keys[14], (MHEADS,), ((0, 4),), -0.4, 0.0), -1.0, 1.0).astype(jnp.bfloat16),
        "gated_gain": jnp.clip(1.0 + 0.1 * jax.random.normal(keys[15], (DS,), jnp.float32), 0.5, 1.5).astype(jnp.bfloat16),
        "merge_weight": gaussian(keys[16], (DS, D), DS ** -0.5, 0.15625, ((0, 4),)),
        "second_gain": jnp.clip(1.0 + 0.1 * jax.random.normal(keys[17], (D,), jnp.float32), 0.5, 1.5).astype(jnp.bfloat16),
        "gate_weight": gaussian(keys[18], (D, FF), D ** -0.5, 0.1875, ((0, 4),)),
        "up_weight": gaussian(keys[19], (D, FF), D ** -0.5, 0.1875, ((0, 4),)),
        "down_weight": gaussian(keys[20], (FF, D), FF ** -0.5, 0.125, ((0, 4),)),
    }


EPSILON = 1e-05
ROPE_BASE = 10000.0
SCORE_SCALE = 0.125
PRECISE = lax.Precision.HIGHEST

@jax.custom_vjp
def low(v):
    return lax.optimization_barrier(v.astype(jnp.bfloat16)).astype(jnp.float32)

@jax.custom_vjp
def low_back(v):
    return v

def low_keep(v):
    return (low(v), None)

def low_pass(kept, grad):
    return (grad,)

def back_keep(v):
    return (v, None)

def back_low(kept, grad):
    return (low(grad),)
low.defvjp(low_keep, low_pass)
low_back.defvjp(back_keep, back_low)

def product(left, right):
    return jnp.dot(left, right, precision=PRECISE, preferred_element_type=jnp.float32)

def root_norm(values, gain):
    return values * lax.rsqrt(lax.optimization_barrier(jnp.mean(values * values, axis=-1, keepdims=True)) + EPSILON) * gain

def rotate(heads, places):
    half_dim = heads.shape[-1] // 2
    freqs = ROPE_BASE ** (-2.0 * jnp.arange(half_dim, dtype=jnp.float32) / heads.shape[-1])
    angles = places.astype(jnp.float32)[:, None] * freqs[None, :]
    cosine = jnp.cos(angles)[:, None, :]
    sine = jnp.sin(angles)[:, None, :]
    front = heads[..., :half_dim]
    behind = heads[..., half_dim:]
    return jnp.concatenate([front * cosine - behind * sine, behind * cosine + front * sine], axis=-1)

def block_decays(log_decay, segment):
    cumulate = jnp.cumsum(log_decay, axis=0)
    ordinal = jnp.arange(segment.shape[0], dtype=jnp.int32)
    related = (segment[:, None] == segment[None, :]) & (ordinal[:, None] >= ordinal[None, :])
    log_gap = jnp.where(related[:, :, None], cumulate[:, None, :] - cumulate[None, :, :], 0.0)
    return (cumulate, jnp.where(related[:, :, None], jnp.exp(log_gap), 0.0))

def block_state(ssm_input, in_matrix, step_size, log_decay, segment, prior_segment):
    cumulate = jnp.cumsum(log_decay, axis=0)
    tail_decay = jnp.where((segment == segment[-1])[:, None], jnp.exp(cumulate[-1][None, :] - cumulate), 0.0) * step_size
    local_state = jnp.einsum('jh,jhp,jn->hpn', tail_decay, ssm_input, in_matrix, precision=PRECISE)
    through = jnp.where(segment[-1] == prior_segment, jnp.exp(cumulate[-1]), 0.0)
    return (through, local_state)

def block_output(ssm_state, ssm_input, in_matrix, out_matrix, step_size, log_decay, segment, prior_segment):
    cumulate, decays = block_decays(log_decay, segment)
    intersection = jnp.dot(out_matrix, in_matrix.T, precision=PRECISE)
    mixing = decays * intersection[:, :, None] * step_size[None, :, :]
    result = jnp.einsum('ijh,jhp->ihp', mixing, ssm_input, precision=PRECISE)
    carry_in = jnp.where((segment == prior_segment)[:, None], jnp.exp(cumulate), 0.0)
    return result + carry_in[:, :, None] * jnp.einsum('in,hpn->ihp', out_matrix, ssm_state, precision=PRECISE)

def attention(queries, key_rows, value_rows, segment):
    length = queries.shape[0]
    block_rows = math.gcd(512, length)
    group_size = QHEADS // KVHEADS
    key_full = jnp.repeat(key_rows, group_size, axis=1)
    value_full = jnp.repeat(value_rows, group_size, axis=1)
    places = jnp.arange(length, dtype=jnp.int32)

    def one_block(index):
        start_row = index * block_rows
        query_block = lax.dynamic_slice_in_dim(queries, start_row, block_rows, 0)
        segment_block = lax.dynamic_slice_in_dim(segment, start_row, block_rows, 0)
        place_block = lax.dynamic_slice_in_dim(places, start_row, block_rows, 0)
        raw_scores = low_back(jnp.einsum('qhd,khd->hqk', query_block, key_full, precision=PRECISE) * SCORE_SCALE)
        allowed = (segment_block[:, None] == segment[None, :]) & (place_block[:, None] >= places[None, :])
        masked = jnp.where(allowed[None], raw_scores, -1e+30)
        highest = lax.optimization_barrier(jnp.max(masked, axis=-1, keepdims=True))
        weights = jnp.exp(masked - highest)
        probability = low(weights / lax.optimization_barrier(jnp.sum(weights, axis=-1, keepdims=True)))
        mixed = jnp.einsum('hqk,khd->qhd', probability, value_full, precision=PRECISE)
        return mixed.reshape(block_rows, QHEADS * HEAD)
    blocks = lax.map(jax.checkpoint(one_block), jnp.arange(length // block_rows, dtype=jnp.int32))
    return blocks.reshape(length, QHEADS * HEAD)

def mamba_mixer(projected, step_raw, segment, conv_weight, conv_bias, step_offset, decay_rate, skip_weight, gated_gain):
    length = projected.shape[0]
    mixer_gate = projected[:, :DS]
    conv_input = projected[:, DS:]
    summed = conv_input * conv_weight[CONVW - 1]
    for offset in range(1, CONVW):
        earlier = jnp.pad(conv_input, ((offset, 0), (0, 0)))[:length]
        segment_earlier = jnp.pad(segment, (offset, 0), constant_values=-1)[:length]
        summed = summed + jnp.where((segment_earlier == segment)[:, None], earlier, 0.0) * conv_weight[CONVW - 1 - offset]
    activated = jax.nn.silu(summed + conv_bias)
    ssm_input = activated[:, :DS].reshape(length, MHEADS, MHEAD)
    in_matrix = activated[:, DS:DS + STATE]
    out_matrix = activated[:, DS + STATE:]
    step_size = jax.nn.softplus(step_raw + step_offset)
    log_decay = -step_size * decay_rate
    blocks = length // STRETCH
    prior = jnp.concatenate([jnp.full((1,), -1, jnp.int32), segment[STRETCH - 1:length - 1:STRETCH]])

    def to_blocks(values):
        return values.reshape((blocks, STRETCH) + values.shape[1:])

    def advance(ssm_state, pieces):
        input_block, in_block, out_block, step_block, decay_block, segment_block, prior_block = pieces
        through, local_state = block_state(input_block, in_block, step_block, decay_block, segment_block, prior_block)
        result = block_output(ssm_state, input_block, in_block, out_block, step_block, decay_block, segment_block, prior_block)
        return (through[:, None, None] * ssm_state + local_state, result)
    start_state = jnp.zeros((MHEADS, MHEAD, STATE), jnp.float32)
    _, outputs = lax.scan(jax.checkpoint(advance), start_state, (to_blocks(ssm_input), to_blocks(in_matrix), to_blocks(out_matrix), to_blocks(step_size), to_blocks(log_decay), to_blocks(segment), prior))
    ssm_out = outputs.reshape(length, MHEADS, MHEAD) + skip_weight[None, :, None] * ssm_input
    gated_out = ssm_out.reshape(length, DS) * jax.nn.silu(mixer_gate)
    return root_norm(gated_out, gated_gain)

def forward(tokens, segment, params):
    entry_gain, query_weight, key_weight, value_weight, output_weight, mixer_weight, step_weight, conv_weight, conv_bias, step_offset, decay_rate, skip_weight, gated_gain, merge_weight, second_gain, gate_weight, up_weight, down_weight = params
    length = tokens.shape[0]
    places = jnp.arange(length, dtype=jnp.int32)
    normed = low(root_norm(tokens, entry_gain))
    queries = low(rotate(low_back(product(normed, query_weight)).reshape(length, QHEADS, HEAD), places))
    key_rows = low(rotate(low_back(product(normed, key_weight)).reshape(length, KVHEADS, HEAD), places))
    value_rows = low(low_back(product(normed, value_weight)).reshape(length, KVHEADS, HEAD))
    attended = attention(queries, key_rows, value_rows, segment)
    attn_branch = low_back(product(low(low_back(attended)), output_weight))
    projected = low_back(product(normed, mixer_weight))
    step_raw = low_back(product(normed, step_weight))
    mixed = mamba_mixer(projected, step_raw, segment, conv_weight, conv_bias, step_offset, decay_rate, skip_weight, gated_gain)
    mamba_branch = low_back(product(low(low_back(mixed)), merge_weight))
    middle = tokens + attn_branch + mamba_branch
    second = low(root_norm(middle, second_gain))
    gate_proj = low_back(product(second, gate_weight))
    up_proj = low_back(product(second, up_weight))
    hidden = low(jax.nn.silu(gate_proj) * up_proj)
    return middle + product(hidden, down_weight)

def reference(hidden_in, cotangent, segments, entry_gain, query_weight, key_weight, value_weight, output_weight, mixer_weight, step_weight, conv_weight, conv_bias, step_offset, decay_rate, skip_weight, gated_gain, merge_weight, second_gain, gate_weight, up_weight, down_weight):
    params = tuple((weight.astype(jnp.float32) for weight in (entry_gain, query_weight, key_weight, value_weight, output_weight, mixer_weight, step_weight, conv_weight, conv_bias, step_offset, decay_rate, skip_weight, gated_gain, merge_weight, second_gain, gate_weight, up_weight, down_weight)))

    def one_sequence(gradients, pieces):
        tokens, segment, incoming = pieces

        def run(inputs, weights):
            return forward(inputs, segment, weights)
        output, pullback = jax.vjp(run, tokens.astype(jnp.float32), params)
        token_delta, param_delta = pullback(incoming.astype(jnp.float32))
        gradients = jax.tree.map(jnp.add, gradients, param_delta)
        return (gradients, (output, token_delta))
    zeroes = tuple((jnp.zeros_like(weight) for weight in params))
    gradients, outputs = lax.scan(one_sequence, zeroes, (hidden_in, segments, cotangent))
    block_out, tokens_grad = outputs
    entry_grad, query_grad, key_grad, value_grad, output_grad, mixer_grad, step_grad, conv_grad, bias_grad, offset_grad, decay_grad, skip_grad, gated_grad, merge_grad, second_grad, gate_grad, up_grad, down_grad = gradients
    return (block_out, tokens_grad, entry_grad, query_grad, key_grad, value_grad, output_grad, mixer_grad, step_grad, conv_grad, bias_grad, offset_grad, decay_grad, skip_grad, gated_grad, merge_grad, second_grad, gate_grad, up_grad, down_grad)
```

```python
import jax
import jax.numpy as jnp
from jax import lax
from jax.experimental import pallas as pl
from jax.experimental.pallas import tpu as pltpu
from jax.sharding import PartitionSpec as P

QHEADS = 8
KVHEADS = 2
HEAD = 64
MHEADS = 24
MHEAD = 64
STATE = 128
CONVW = 4
QW = 512
KW = 128
DS = 1536
PROJ = 3328


EPSILON = 1e-05
ROPE_BASE = 10000.0
SCORE_SCALE = 0.125
PRECISE = lax.Precision.HIGH
LANES = 128
VMEM_BYTES = 48 * 1024 * 1024


def shifted(block, axis, distance):
    devices = range(lax.axis_size(axis))
    route = [(i - distance, i) for i in devices if i - distance in devices]
    return lax.ppermute(block, axis, route)


def states_before(through_all, states_all, axis):
    count, mine = (states_all.shape[0], lax.axis_index(axis))
    order = jnp.arange(count)
    between = (order[None, :] > order[:, None]) & (order[None, :] < mine)
    factors = jnp.where(between[:, :, None, None], through_all[None], 1.0)
    weights = jnp.where((order < mine)[:, None, None], jnp.prod(factors, axis=1), 0.0)
    return jnp.sum(weights[..., None, None] * states_all.astype(jnp.float32), axis=0)


def states_after(through_all, states_all, axis):
    count, mine = (states_all.shape[0], lax.axis_index(axis))
    order = jnp.arange(count)
    between = (order[None, :] < order[:, None]) & (order[None, :] > mine)
    factors = jnp.where(between[:, :, None, None], through_all[None], 1.0)
    weights = jnp.where((order > mine)[:, None, None], jnp.prod(factors, axis=1), 0.0)
    return jnp.sum(weights[..., None, None] * states_all.astype(jnp.float32), axis=0)


def matmul(left, right):
    return jnp.dot(left, right, preferred_element_type=jnp.float32)


def weight_grad(left, right):
    return jnp.einsum("rd,rf->df", left, right, preferred_element_type=jnp.float32)


def back_product(grads_in, weight):
    return jnp.einsum("rf,df->rd", grads_in, weight, preferred_element_type=jnp.float32)


def root_norm(values, gain):
    return values * lax.rsqrt(jnp.mean(values * values, axis=-1, keepdims=True) + EPSILON) * gain


def rotate(heads, places):
    half_dim = heads.shape[-1] // 2
    freqs = ROPE_BASE ** (-2.0 * jnp.arange(half_dim, dtype=jnp.float32) / heads.shape[-1])
    angles = places.astype(jnp.float32)[:, None] * freqs[None, :]
    cosine = jnp.cos(angles)[:, None, :]
    sine = jnp.sin(angles)[:, None, :]
    front = heads[..., :half_dim]
    behind = heads[..., half_dim:]
    return jnp.concatenate(
        [front * cosine - behind * sine, behind * cosine + front * sine], axis=-1
    )


def block_decays(log_decay, segment):
    cumulate = jnp.cumsum(log_decay, axis=0)
    ordinal = jnp.arange(segment.shape[0], dtype=jnp.int32)
    related = (segment[:, None] == segment[None, :]) & (ordinal[:, None] >= ordinal[None, :])
    log_gap = jnp.where(related[:, :, None], cumulate[:, None, :] - cumulate[None, :, :], 0.0)
    return (cumulate, jnp.where(related[:, :, None], jnp.exp(log_gap), 0.0))


def block_state(ssm_input, in_matrix, step_size, log_decay, segment, prior_segment):
    cumulate = jnp.cumsum(log_decay, axis=0)
    tail_decay = (
        jnp.where((segment == segment[-1])[:, None], jnp.exp(cumulate[-1][None, :] - cumulate), 0.0)
        * step_size
    )
    local_state = jnp.einsum("jh,jhp,jn->hpn", tail_decay, ssm_input, in_matrix, precision=PRECISE)
    through = jnp.where(segment[-1] == prior_segment, jnp.exp(cumulate[-1]), 0.0)
    return (through, local_state)


def block_output(
    ssm_state, ssm_input, in_matrix, out_matrix, step_size, log_decay, segment, prior_segment
):
    cumulate, decays = block_decays(log_decay, segment)
    intersection = jnp.dot(out_matrix, in_matrix.T, precision=PRECISE)
    mixing = decays * intersection[:, :, None] * step_size[None, :, :]
    result = jnp.einsum("ijh,jhp->ihp", mixing, ssm_input, precision=PRECISE)
    carry_in = jnp.where((segment == prior_segment)[:, None], jnp.exp(cumulate), 0.0)
    return result + carry_in[:, :, None] * jnp.einsum(
        "in,hpn->ihp", out_matrix, ssm_state, precision=PRECISE
    )


def mamba_front(
    projected,
    rim_rows,
    step_raw,
    segment_ext,
    prior_segment,
    conv_taps,
    conv_shift,
    step_shift,
    decay_speed,
):
    length = projected.shape[0]
    back_reach = CONVW - 1
    conv_input = jnp.concatenate([rim_rows, projected[:, DS:]], axis=0)
    segment = segment_ext[back_reach:]
    summed = conv_input[back_reach:] * conv_taps[back_reach]
    for offset in range(1, CONVW):
        start_row = back_reach - offset
        earlier = conv_input[start_row : start_row + length]
        related = segment_ext[start_row : start_row + length] == segment
        summed = summed + jnp.where(related[:, None], earlier, 0.0) * conv_taps[start_row]
    activated = jax.nn.silu(summed + conv_shift)
    ssm_input = activated[:, :DS].reshape(length, MHEADS, MHEAD)
    in_matrix = activated[:, DS : DS + STATE]
    out_matrix = activated[:, DS + STATE :]
    step_size = jax.nn.softplus(step_raw + step_shift)
    log_decay = -step_size * decay_speed
    chain = block_state(ssm_input, in_matrix, step_size, log_decay, segment, prior_segment)
    return ((ssm_input, in_matrix, out_matrix, step_size, log_decay), chain)


def mamba_tail(ssm_state, inside, mixer_gate, segment, prior_segment, skip_scale, gated_scale):
    ssm_input, in_matrix, out_matrix, step_size, log_decay = inside
    length = mixer_gate.shape[0]
    ssm_out = (
        block_output(
            ssm_state,
            ssm_input,
            in_matrix,
            out_matrix,
            step_size,
            log_decay,
            segment,
            prior_segment,
        )
        + skip_scale[None, :, None] * ssm_input
    )
    gated_out = ssm_out.reshape(length, DS) * jax.nn.silu(mixer_gate)
    return root_norm(gated_out, gated_scale)


def dot_nn(left, right):
    return jnp.dot(left, right, preferred_element_type=jnp.float32)


def dot_nt(left, right):
    return lax.dot_general(
        left, right, (((1,), (1,)), ((), ())), preferred_element_type=jnp.float32
    )


def masked_scores(key_ref, query_ref, low_ref, high_ref):
    raw_scores = dot_nt(key_ref[0, 0], query_ref[0, 0]) * SCORE_SCALE
    places = lax.broadcasted_iota(jnp.int32, raw_scores.shape, 0)
    allowed = (places >= low_ref[0]) & (places <= high_ref[0])
    return jnp.where(allowed, raw_scores, -1e30)


def attend_forward_kernel(
    low_ref, high_ref, query_ref, key_ref, value_t_ref, out_ref, highest_ref, total_ref
):
    masked = masked_scores(key_ref, query_ref, low_ref, high_ref)
    highest = jnp.max(masked, axis=0, keepdims=True)
    weights = jnp.exp(masked - highest)
    total = jnp.sum(weights, axis=0, keepdims=True)
    probability = (weights * (1.0 / total)).astype(jnp.bfloat16)
    out_ref[0, 0] = dot_nn(value_t_ref[0, 0], probability)
    highest_ref[0, 0] = highest
    total_ref[0, 0] = total


def attend_backward_kernel(
    group_size,
    low_ref,
    high_ref,
    query_ref,
    delta_ref,
    key_ref,
    value_ref,
    key_t_ref,
    highest_ref,
    total_ref,
    centre_ref,
    query_out,
    key_out,
    value_out,
):
    masked = masked_scores(key_ref, query_ref, low_ref, high_ref)
    probability = jnp.exp(masked - highest_ref[0, 0]) * (1.0 / total_ref[0, 0])
    weight_delta = dot_nt(value_ref[0, 0], delta_ref[0, 0])
    score_low = (probability * (weight_delta - centre_ref[0, 0])).astype(jnp.bfloat16)
    query_out[0, 0] = dot_nn(key_t_ref[0, 0], score_low) * SCORE_SCALE
    key_term = dot_nn(score_low, query_ref[0, 0]) * SCORE_SCALE
    value_term = dot_nn(probability.astype(jnp.bfloat16), delta_ref[0, 0])
    first = pl.program_id(1) % group_size == 0

    @pl.when(first)
    def _():
        key_out[0, 0] = key_term
        value_out[0, 0] = value_term

    @pl.when(jnp.logical_not(first))
    def _():
        key_out[0, 0] += key_term
        value_out[0, 0] += value_term


def head_specs(batches, length, seq_span):
    group_size = QHEADS // KVHEADS
    return {
        "low": pl.BlockSpec((1, 1, length), lambda b, h: (b, 0, 0)),
        "high": pl.BlockSpec((1, 1, length), lambda b, h: (0, 0, 0)),
        "query": pl.BlockSpec((1, 1, length, HEAD), lambda b, h: (b, h, 0, 0)),
        "query_t": pl.BlockSpec((1, 1, HEAD, length), lambda b, h: (b, h, 0, 0)),
        "row": pl.BlockSpec((1, 1, 1, length), lambda b, h: (b, h, 0, 0)),
        "key": pl.BlockSpec((1, 1, seq_span, HEAD), lambda b, h: (b, h // group_size, 0, 0)),
        "key_t": pl.BlockSpec((1, 1, HEAD, seq_span), lambda b, h: (b, h // group_size, 0, 0)),
    }


def attend_forward(low, high, query_heads, key_heads, value_heads_t):
    batches, _, length, _ = query_heads.shape
    seq_span = key_heads.shape[2]
    specs = head_specs(batches, length, seq_span)
    return pl.pallas_call(
        attend_forward_kernel,
        grid=(batches, QHEADS),
        in_specs=[specs[name] for name in ("low", "high", "query", "key", "key_t")],
        out_specs=[specs["query_t"], specs["row"], specs["row"]],
        out_shape=[
            jax.ShapeDtypeStruct((batches, QHEADS, HEAD, length), jnp.float32),
            jax.ShapeDtypeStruct((batches, QHEADS, 1, length), jnp.float32),
            jax.ShapeDtypeStruct((batches, QHEADS, 1, length), jnp.float32),
        ],
        compiler_params=pltpu.CompilerParams(vmem_limit_bytes=VMEM_BYTES),
        cost_estimate=pl.CostEstimate(
            flops=8 * batches * QHEADS * length * seq_span * HEAD,
            bytes_accessed=24 * batches * seq_span * LANES,
            transcendentals=batches * QHEADS * length * seq_span,
        ),
    )(low, high, query_heads, key_heads, value_heads_t)


def attend_backward(
    low, high, query_heads, delta_heads, key_heads, value_heads, key_heads_t, highest, total, centre
):
    batches, _, length, _ = query_heads.shape
    seq_span = key_heads.shape[2]
    specs = head_specs(batches, length, seq_span)
    names = ("low", "high", "query", "query", "key", "key", "key_t", "row", "row", "row")

    def kernel(*refs):
        attend_backward_kernel(QHEADS // KVHEADS, *refs)

    return pl.pallas_call(
        kernel,
        grid=(batches, QHEADS),
        in_specs=[specs[name] for name in names],
        out_specs=[specs["query_t"], specs["key"], specs["key"]],
        out_shape=[
            jax.ShapeDtypeStruct((batches, QHEADS, HEAD, length), jnp.float32),
            jax.ShapeDtypeStruct((batches, KVHEADS, seq_span, HEAD), jnp.float32),
            jax.ShapeDtypeStruct((batches, KVHEADS, seq_span, HEAD), jnp.float32),
        ],
        compiler_params=pltpu.CompilerParams(vmem_limit_bytes=VMEM_BYTES),
        cost_estimate=pl.CostEstimate(
            flops=20 * batches * QHEADS * length * seq_span * HEAD,
            bytes_accessed=48 * batches * seq_span * LANES,
            transcendentals=batches * QHEADS * length * seq_span,
        ),
    )(
        low,
        high,
        query_heads,
        delta_heads,
        key_heads,
        value_heads,
        key_heads_t,
        highest,
        total,
        centre,
    )


def gather_rows(*shards):
    count, mine = (lax.axis_size("ctx"), lax.axis_index("ctx"))
    pieces = [
        lax.dynamic_slice_in_dim(shard, mine * (shard.shape[0] // count), shard.shape[0] // count, 0)
        for shard in shards
    ]
    width = sum(piece.shape[1] for piece in pieces)
    if width % LANES:
        pieces.append(jnp.zeros((pieces[0].shape[0], LANES - width % LANES), pieces[0].dtype))
    joined = jnp.concatenate(pieces, axis=1) if len(pieces) > 1 else pieces[0]
    return lax.all_gather(joined, ("fsdp", "ctx"), axis=0, tiled=True)


def reduce_rows(grads):
    splits, count = (lax.axis_size("fsdp"), lax.axis_size("ctx"))
    blocks = [
        grad.astype(jnp.bfloat16).reshape(splits, count, -1, grad.shape[1]) for grad in grads
    ]
    heights = [block.shape[2] for block in blocks]
    joined = jnp.concatenate(blocks, axis=2) if len(blocks) > 1 else blocks[0]
    width = joined.shape[3]
    joined = joined.transpose(1, 0, 2, 3).reshape(-1, width)
    part = lax.psum_scatter(joined, "ctx", scatter_dimension=0, tiled=True)
    part = lax.psum_scatter(part, "fsdp", scatter_dimension=0, tiled=True)
    rows = lax.all_gather(part, "ctx", axis=0, tiled=True)
    rows = rows.reshape(count, -1, width)
    results, at = ([], 0)
    for height in heights:
        results.append(rows[:, at : at + height].reshape(-1, width).astype(jnp.float32))
        at += height
    return results


def per_device(
    hidden_in,
    cotangent,
    segments,
    entry_gain,
    query_weight,
    key_weight,
    value_weight,
    output_weight,
    mixer_weight,
    step_weight,
    conv_weight,
    conv_bias,
    step_offset,
    decay_rate,
    skip_weight,
    gated_gain,
    merge_weight,
    second_gain,
    gate_weight,
    up_weight,
    down_weight,
):
    splits = lax.axis_size("fsdp")
    narrow = (
        entry_gain,
        conv_weight.reshape(-1),
        conv_bias,
        step_offset,
        decay_rate,
        skip_weight,
        gated_gain,
        second_gain,
    )
    narrow_all = lax.all_gather(jnp.concatenate(narrow), "fsdp", axis=0)
    wide = []
    at = 0
    for piece in narrow:
        wide.append(narrow_all[:, at : at + piece.shape[0]].astype(jnp.float32))
        at += piece.shape[0]
    entry_scale, conv_shift, step_shift, decay_speed, skip_scale, gated_scale, second_scale = [
        wide[i].reshape(-1) for i in (0, 2, 3, 4, 5, 6, 7)
    ]
    conv_taps = wide[1].reshape(splits, CONVW, -1).transpose(1, 0, 2).reshape(CONVW, -1)
    front_full = gather_rows(query_weight, key_weight, value_weight, mixer_weight, step_weight)
    output_full = gather_rows(output_weight)
    merge_full = gather_rows(merge_weight)
    rise_full = gather_rows(gate_weight, up_weight)
    down_full = gather_rows(down_weight)
    batches, length, features = hidden_in.shape
    flat_rows = batches * length
    back_reach = CONVW - 1
    first_proj = QW + 2 * KW
    first_step = first_proj + PROJ
    anchor = lax.axis_index("ctx") * length
    places = anchor + jnp.arange(length, dtype=jnp.int32)
    padded_segments = jnp.concatenate(
        [jnp.full((batches, back_reach), -1, jnp.int32), segments], axis=1
    )
    segment_ext = lax.dynamic_slice_in_dim(padded_segments, anchor, length + back_reach, 1)
    segment_here = segment_ext[:, back_reach:]
    prior_segment = segment_ext[:, back_reach - 1]
    document_start = jnp.sum(
        (segments[:, None, :] < segment_here[:, :, None]).astype(jnp.int32), axis=2
    )[:, None, :]
    place_row = places[None, None, :]
    tokens = hidden_in.reshape(flat_rows, features).astype(jnp.float32)
    normed = root_norm(tokens, entry_scale).astype(jnp.bfloat16)
    front = matmul(normed, front_full)

    def split_heads(rows, count):
        return rows.reshape(batches, -1, count, HEAD).transpose(0, 2, 1, 3)

    queries = split_heads(
        rotate(front[:, :QW].reshape(batches, length, QHEADS, HEAD), places).astype(jnp.bfloat16),
        QHEADS,
    )
    key_rows = (
        rotate(front[:, QW : QW + KW].reshape(batches, length, KVHEADS, HEAD), places)
        .astype(jnp.bfloat16)
        .reshape(batches, length, KW)
    )
    value_rows = front[:, QW + KW : first_proj].astype(jnp.bfloat16).reshape(batches, length, KW)
    all_pairs = lax.all_gather(
        jnp.concatenate([key_rows, value_rows], axis=2), "ctx", axis=1, tiled=True
    )
    key_heads = split_heads(all_pairs[:, :, :KW], KVHEADS)
    value_heads = split_heads(all_pairs[:, :, KW:], KVHEADS)
    attended_t, highest, total = attend_forward(
        document_start, place_row, queries, key_heads, value_heads.swapaxes(2, 3)
    )
    attended_low = (
        attended_t.astype(jnp.bfloat16).transpose(0, 3, 1, 2).reshape(flat_rows, QW)
    )
    projected = front[:, first_proj:first_step].reshape(batches, length, PROJ)
    step_raw = front[:, first_step : first_step + MHEADS].reshape(batches, length, MHEADS)
    rim_rows = shifted(projected[:, length - back_reach :, DS:], "ctx", 1)
    front_map = jax.vmap(mamba_front, in_axes=(0, 0, 0, 0, 0, None, None, None, None))
    tail_map = jax.vmap(mamba_tail, in_axes=(0, 0, 0, 0, 0, None, None))
    inside, chain = front_map(
        projected,
        rim_rows,
        step_raw,
        segment_ext,
        prior_segment,
        conv_taps,
        conv_shift,
        step_shift,
        decay_speed,
    )
    through_decay, local_state = chain
    through_all = lax.all_gather(through_decay, "ctx")
    state_in = states_before(
        through_all, lax.all_gather(local_state.astype(jnp.bfloat16), "ctx"), "ctx"
    )
    mixer_gate = projected[:, :, :DS]
    mixed = tail_map(
        state_in, inside, mixer_gate, segment_here, prior_segment, skip_scale, gated_scale
    )
    mixed_low = mixed.reshape(flat_rows, DS).astype(jnp.bfloat16)
    middle = tokens + matmul(attended_low, output_full) + matmul(mixed_low, merge_full)
    second = root_norm(middle, second_scale).astype(jnp.bfloat16)
    rise = matmul(second, rise_full)
    half = rise.shape[1] // 2
    gate_proj = rise[:, :half]
    up_proj = rise[:, half:]
    hidden = (jax.nn.silu(gate_proj) * up_proj).astype(jnp.bfloat16)
    block_out = (middle + matmul(hidden, down_full)).reshape(batches, length, features)
    incoming = cotangent.reshape(flat_rows, features)
    (down_sum,) = reduce_rows([weight_grad(hidden, incoming)])
    hidden_delta = back_product(incoming, down_full)
    _, swiglu_pull = jax.vjp(
        lambda gate_in, up_in: jax.nn.silu(gate_in) * up_in, gate_proj, up_proj
    )
    gate_delta, up_delta = swiglu_pull(hidden_delta)
    rise_low = jnp.concatenate([gate_delta, up_delta], axis=1).astype(jnp.bfloat16)
    (rise_sum,) = reduce_rows([weight_grad(second, rise_low)])
    gate_sum = rise_sum[:, :half]
    up_sum = rise_sum[:, half:]
    second_delta = back_product(rise_low, rise_full)
    _, second_pull = jax.vjp(root_norm, middle, second_scale)
    middle_norm_delta, second_grad = second_pull(second_delta)
    middle_delta = incoming.astype(jnp.float32) + middle_norm_delta
    branch_low = middle_delta.astype(jnp.bfloat16)
    output_sum, merge_sum = reduce_rows(
        [weight_grad(attended_low, branch_low), weight_grad(mixed_low, branch_low)]
    )
    attended_delta = back_product(branch_low, output_full).astype(jnp.bfloat16)
    mixed_delta = (
        lax.optimization_barrier(back_product(branch_low, merge_full).astype(jnp.bfloat16))
        .astype(jnp.float32)
        .reshape(batches, length, DS)
    )

    def tail_apply(state_value, inside_value, gate_value, skip_value, gain_value):
        return tail_map(
            state_value,
            inside_value,
            gate_value,
            segment_here,
            prior_segment,
            skip_value,
            gain_value,
        )

    _, tail_pull = jax.vjp(tail_apply, state_in, inside, mixer_gate, skip_scale, gated_scale)
    state_delta, inside_delta, gate_z_delta, skip_grad, gated_grad = tail_pull(mixed_delta)
    carried_delta = states_after(
        through_all, lax.all_gather(state_delta.astype(jnp.bfloat16), "ctx"), "ctx"
    )
    through_delta = jnp.sum(carried_delta * state_in, axis=(2, 3))

    def front_apply(
        proj_value, rim_value, step_value, taps_value, shift_value, offset_value, decay_value
    ):
        return front_map(
            proj_value,
            rim_value,
            step_value,
            segment_ext,
            prior_segment,
            taps_value,
            shift_value,
            offset_value,
            decay_value,
        )

    _, front_pull = jax.vjp(
        front_apply, projected, rim_rows, step_raw, conv_taps, conv_shift, step_shift, decay_speed
    )
    delta_heads = split_heads(attended_delta, QHEADS)
    centre = jnp.sum(
        attended_t * delta_heads.astype(jnp.float32).swapaxes(2, 3), axis=2, keepdims=True
    )
    query_delta_t, key_part, value_part = attend_backward(
        document_start,
        place_row,
        queries,
        delta_heads,
        key_heads,
        value_heads,
        key_heads.swapaxes(2, 3),
        highest,
        total,
        centre,
    )
    pair_delta = lax.psum_scatter(
        jnp.concatenate([key_part, value_part], axis=1)
        .astype(jnp.bfloat16)
        .transpose(2, 0, 1, 3)
        .reshape(-1, batches * 2 * KW),
        "ctx",
        scatter_dimension=0,
        tiled=True,
    )
    pair_delta = (
        pair_delta.astype(jnp.float32).reshape(length, batches, 2 * KW).swapaxes(0, 1)
    )
    key_low = (
        rotate(pair_delta[:, :, :KW].reshape(batches, length, KVHEADS, HEAD), -places)
        .astype(jnp.bfloat16)
        .reshape(flat_rows, KW)
    )
    value_low = pair_delta[:, :, KW:].astype(jnp.bfloat16).reshape(flat_rows, KW)
    query_low = (
        rotate(query_delta_t.transpose(0, 3, 1, 2), -places)
        .astype(jnp.bfloat16)
        .reshape(flat_rows, QW)
    )
    early_low = jnp.concatenate(
        [
            query_low,
            key_low,
            value_low,
            gate_z_delta.astype(jnp.bfloat16).reshape(flat_rows, DS),
        ],
        axis=1,
    )
    (early_sum,) = reduce_rows([weight_grad(normed, early_low)])
    query_sum = early_sum[:, :QW]
    key_sum = early_sum[:, QW : QW + KW]
    value_sum = early_sum[:, QW + KW : first_proj]
    proj_delta, rim_delta, step_delta, conv_grad, bias_grad, offset_grad, decay_grad = front_pull(
        (inside_delta, (through_delta, carried_delta))
    )
    rim_back = shifted(rim_delta, "ctx", -1)
    conv_delta = proj_delta[:, :, DS:].at[:, length - back_reach :].add(rim_back)
    late_low = jnp.concatenate(
        [
            conv_delta.reshape(flat_rows, PROJ - DS),
            step_delta.reshape(flat_rows, MHEADS),
            jnp.zeros((flat_rows, front_full.shape[1] - first_step - MHEADS), jnp.float32),
        ],
        axis=1,
    ).astype(jnp.bfloat16)
    (late_sum,) = reduce_rows([weight_grad(normed, late_low)])
    mixer_sum = jnp.concatenate([early_sum[:, first_proj:], late_sum[:, : PROJ - DS]], axis=1)
    step_sum = late_sum[:, PROJ - DS : PROJ - DS + MHEADS]
    early_width = early_low.shape[1]
    normed_delta = back_product(early_low, front_full[:, :early_width]) + back_product(
        late_low, front_full[:, early_width:]
    )
    _, entry_pull = jax.vjp(root_norm, tokens, entry_scale)
    token_delta, entry_grad = entry_pull(normed_delta)
    tokens_grad = (middle_delta + token_delta).reshape(batches, length, features)
    slight = (
        entry_grad,
        conv_grad.reshape(-1),
        bias_grad,
        offset_grad,
        decay_grad,
        skip_grad,
        gated_grad,
        second_grad,
    )
    slight_all = lax.psum(jnp.concatenate(slight), ("fsdp", "ctx"))
    sums = []
    at = 0
    for index, piece in enumerate(slight):
        whole = slight_all[at : at + piece.shape[0]]
        at += piece.shape[0]
        whole = whole.reshape((CONVW, -1) if index == 1 else (1, -1))
        share = whole.shape[1] // splits
        own = lax.dynamic_slice_in_dim(whole, lax.axis_index("fsdp") * share, share, 1)
        sums.append(own if index == 1 else own.reshape(-1))
    entry_sum, conv_sum, bias_sum, offset_sum, decay_sum, skip_sum, gated_sum, second_sum = sums
    return (
        block_out,
        tokens_grad,
        entry_sum,
        query_sum,
        key_sum,
        value_sum,
        output_sum,
        mixer_sum,
        step_sum,
        conv_sum,
        bias_sum,
        offset_sum,
        decay_sum,
        skip_sum,
        gated_sum,
        merge_sum,
        second_sum,
        gate_sum,
        up_sum,
        down_sum,
    )


def solution(mesh):
    placed = (
        P("fsdp", "ctx", None),
        P("fsdp", "ctx", None),
        P("fsdp", None),
        P("fsdp"),
        P("fsdp", None),
        P("fsdp", None),
        P("fsdp", None),
        P("fsdp", None),
        P("fsdp", None),
        P("fsdp", None),
        P(None, "fsdp"),
        P("fsdp"),
        P("fsdp"),
        P("fsdp"),
        P("fsdp"),
        P("fsdp"),
        P("fsdp", None),
        P("fsdp"),
        P("fsdp", None),
        P("fsdp", None),
        P("fsdp", None),
    )
    return jax.shard_map(
        per_device,
        mesh=mesh,
        in_specs=placed,
        out_specs=(
            P("fsdp", "ctx", None),
            P("fsdp", "ctx", None),
            P("fsdp"),
            P("fsdp", None),
            P("fsdp", None),
            P("fsdp", None),
            P("fsdp", None),
            P("fsdp", None),
            P("fsdp", None),
            P(None, "fsdp"),
            P("fsdp"),
            P("fsdp"),
            P("fsdp"),
            P("fsdp"),
            P("fsdp"),
            P("fsdp", None),
            P("fsdp"),
            P("fsdp", None),
            P("fsdp", None),
            P("fsdp", None),
        ),
        check_vma=False,
    )
```
